32 devices in a mesh: groups: 2 (over y), lat: 16 (over z, x, core).
Axes of the slice: x: 2, y: 2, z: 4, core: 2. Of those that a mesh axis runs over, the one named last changes fastest.
Arguments:
- grid_lat: bfloat16 [65536, 512], P(('groups', 'lat')), parts along dimension 0, may hold values from -6 to 6
- mesh_lat: bfloat16 [4096, 512], P(('groups', 'lat')), parts along dimension 0, may hold values from -6 to 6
- enc_feat: bfloat16 [4, 131072], P(None, ('groups', 'lat')), parts along dimension 1, may hold values from -5 to 5
- enc_src: int32 [131072], P(('groups', 'lat')), parts along dimension 0, may hold values from 0 to 2047
- enc_dst: int32 [131072], P(('groups', 'lat')), parts along dimension 0, may hold values from 0 to 383, as said below
- mesh_send: int32 [32, 16, 8], P(('groups', 'lat')), parts along dimension 0, may hold values from 0 to 127
- mesh_senders: int32 [65536], P(('groups', 'lat')), parts along dimension 0, may hold values from 0 to 255, as said below
- mesh_recv: int32 [65536], P(('groups', 'lat')), parts along dimension 0, may hold values from 0 to 127
- w_enc_grid: bfloat16 [512, 512], replicated, may hold values from -0.25 to 0.25
- w_enc_feat: bfloat16 [4, 512], replicated, may hold values from -3 to 3
- b_enc: float32 [512], replicated, may hold values from -3 to 3
- w_enc_out: bfloat16 [512, 512], replicated, may hold values from -0.25 to 0.25
- b_enc_out: float32 [512], replicated, may hold values from -3 to 3
- w_node_self: bfloat16 [512, 512], replicated, may hold values from -0.25 to 0.25
- w_node_agg: bfloat16 [512, 512], replicated, may hold values from -0.09375 to 0.09375
- b_node: float32 [512], replicated, may hold values from -3 to 3
- w_node_out: bfloat16 [512, 512], replicated, may hold values from -0.25 to 0.25
- b_node_out: float32 [512], replicated, may hold values from -3 to 3
- gain_node: float32 [512], replicated, may hold values from 0.25 to 1.75
- w_edge_send: bfloat16 [512, 512], replicated, may hold values from -0.25 to 0.25
- w_edge_recv: bfloat16 [512, 512], replicated, may hold values from -0.25 to 0.25
- b_edge: float32 [512], replicated, may hold values from -3 to 3
- w_edge_out: bfloat16 [512, 512], replicated, may hold values from -0.25 to 0.25
- b_edge_out: float32 [512], replicated, may hold values from -1.2 to 1.2
- w_proc_self: bfloat16 [512, 512], replicated, may hold values from -0.25 to 0.25
- w_proc_agg: bfloat16 [512, 512], replicated, may hold values from -0.1875 to 0.1875
- b_proc: float32 [512], replicated, may hold values from -3 to 3
- w_proc_out: bfloat16 [512, 512], replicated, may hold values from -0.25 to 0.25
- b_proc_out: float32 [512], replicated, may hold values from -3 to 3
- gain_proc: float32 [512], replicated, may hold values from 0.25 to 1.75
Outputs:
- mesh_out: bfloat16 [4096, 512], P(('groups', 'lat')), parts along dimension 0
The draws below stay inside these ranges and needn't reach their ends.
There are 2 independent parts, one for each index of `groups`. The reference program is written for one: setup_inputs(seed, part) draws one part's arguments, and reference() takes and returns one part's arrays. A program takes and returns all parts, laid end to end along the dimension named above; an argument that names none is the same for every part. Nothing has to cross between parts.
Inputs may be any that keep to these rules, and one draw needn't show every extreme that they name: `enc_dst`: band 0 has no key below 128 and the last band none at or above 256. `mesh_senders`: on each patch every one of the 128 handed-over slots is the sender of at least one edge.
All inputs are finite; a program needn't handle non-finite values.
Results may differ from the reference program's by a relative error of at most 0.009.
Values may be sent and summed in bfloat16 or wider, within the bound.
A program may use at most 128 MiB of HBM per device.

```python
import jax
import jax.numpy as jnp
from jax import lax

D = 512
FEAT = 4
G_DEV = 2048
M_DEV = 128
ME_DEV = 2048
CAP = 8
ENC_DEV = 4096
GRID = 32768
MESH = 2048
ENC = 65536
MEDGES = 32768
N_LAT = 16


def draw_enc_dst(key, part):
    key = jax.random.fold_in(key, 3)
    key_offset, key_row = jax.random.split(key)
    band = jnp.arange(ENC, dtype=jnp.int32) // ENC_DEV
    offset = jax.random.randint(key_offset, (ENC,), 0, 3, dtype=jnp.int32)
    offset = jnp.where((band == 0) & (offset == 0), 1, offset)
    offset = jnp.where((band == N_LAT - 1) & (offset == 2), 1, offset)
    row_index = jax.random.randint(key_row, (ENC,), 0, M_DEV, dtype=jnp.int32)
    row_index = row_index.at[ENC_DEV].set(M_DEV - 1)
    offset = offset.at[ENC_DEV].set(2)
    offset = offset.at[ENC_DEV + 1].set(0)
    return offset * M_DEV + row_index


def draw_mesh_senders(key, part):
    key = jax.random.fold_in(key, 7)
    slots = N_LAT * CAP
    patch_keys = jax.random.split(key, N_LAT)

    def one_patch(patch_key):
        key_first, key_rest, key_order = jax.random.split(patch_key, 3)
        first = M_DEV + jax.random.permutation(key_first, slots).astype(jnp.int32)
        others = jax.random.randint(key_rest, (ME_DEV - slots,), 0, M_DEV + slots, dtype=jnp.int32)
        return jax.random.permutation(key_order, jnp.concatenate([first, others]))
    return jax.vmap(one_patch)(patch_keys).reshape(-1)


def with_ends(result, key, smallest, top_value):
    dims = result.shape
    place = [jax.random.randint(jax.random.fold_in(key, axis), (), 0, dims[axis]) for axis in range(len(dims))]
    result = result.at[tuple(place)].set(smallest)
    longest = dims.index(max(dims))
    place[longest] = (place[longest] + 1) % dims[longest]
    return result.at[tuple(place)].set(top_value)


def shard_levels(rng, dims, cuts, least, high):
    factor_of, own = 1.0, jax.random.fold_in(rng, 6)
    for position, shards_of in cuts:
        heights = jnp.exp(jax.random.uniform(jax.random.fold_in(own, position), (shards_of,), jnp.float32, least / len(cuts), high / len(cuts)))
        factor_of = factor_of * jnp.repeat(heights, dims[position] // shards_of).reshape([-1 if axis == position else 1 for axis in range(len(dims))])
    return factor_of


def normal_values(stream_key, dims, width, most, pieces=(), held_as=jnp.bfloat16):
    entries = width * jax.random.normal(stream_key, dims, jnp.float32)
    if pieces:
        entries = entries * shard_levels(stream_key, dims, pieces, -0.22, 0.18)
    return jnp.clip(entries, -most, most).astype(held_as)


def setup_inputs(seed: int = 0, part: int = 0) -> dict:
    key_list = jax.random.split(jax.random.key(seed), 31)
    part_keys = jax.random.split(jax.random.fold_in(key_list[30], part), 31)
    return {
        "grid_lat": normal_values(part_keys[0], (GRID, D), 1.0, 6.0, ((0, 16),)),
        "mesh_lat": normal_values(part_keys[1], (MESH, D), 1.0, 6.0, ((0, 16),)),
        "enc_feat": normal_values(part_keys[2], (FEAT, ENC), 1.0, 5.0, ((1, 16),)),
        "enc_src": with_ends(jax.random.randint(part_keys[3], (ENC,), 0, G_DEV), jax.random.fold_in(part_keys[3], 1), 0, G_DEV - 1).astype(jnp.int32),
        "enc_dst": draw_enc_dst(jax.random.fold_in(jax.random.fold_in(key_list[30], part), 71), part),
        "mesh_send": with_ends(jax.random.randint(part_keys[5], (N_LAT, N_LAT, CAP), 0, M_DEV), jax.random.fold_in(part_keys[5], 1), 0, M_DEV - 1).astype(jnp.int32),
        "mesh_senders": draw_mesh_senders(jax.random.fold_in(jax.random.fold_in(key_list[30], part), 71), part),
        "mesh_recv": with_ends(jax.random.randint(part_keys[7], (MEDGES,), 0, M_DEV), jax.random.fold_in(part_keys[7], 1), 0, M_DEV - 1).astype(jnp.int32),
        "w_enc_grid": normal_values(key_list[8], (D, D), D ** -0.5, 0.25),
        "w_enc_feat": normal_values(key_list[9], (FEAT, D), FEAT ** -0.5, 3.0),
        "b_enc": normal_values(key_list[10], (D,), 0.5, 3.0, (), jnp.float32),
        "w_enc_out": normal_values(key_list[11], (D, D), D ** -0.5, 0.25),
        "b_enc_out": normal_values(key_list[12], (D,), 0.5, 3.0, (), jnp.float32),
        "w_node_self": normal_values(key_list[13], (D, D), D ** -0.5, 0.25),
        "w_node_agg": normal_values(key_list[14], (D, D), (8 * D) ** -0.5, 0.09375),
        "b_node": normal_values(key_list[15], (D,), 0.5, 3.0, (), jnp.float32),
        "w_node_out": normal_values(key_list[16], (D, D), D ** -0.5, 0.25),
        "b_node_out": normal_values(key_list[17], (D,), 0.5, 3.0, (), jnp.float32),
        "gain_node": jnp.clip(1.0 + 0.15 * jax.random.normal(key_list[18], (D,), jnp.float32), 0.25, 1.75),
        "w_edge_send": normal_values(key_list[19], (D, D), D ** -0.5, 0.25),
        "w_edge_recv": normal_values(key_list[20], (D, D), D ** -0.5, 0.25),
        "b_edge": normal_values(key_list[21], (D,), 0.5, 3.0, (), jnp.float32),
        "w_edge_out": normal_values(key_list[22], (D, D), D ** -0.5, 0.25),
        "b_edge_out": normal_values(key_list[23], (D,), 0.2, 1.2, (), jnp.float32),
        "w_proc_self": normal_values(key_list[24], (D, D), D ** -0.5, 0.25),
        "w_proc_agg": normal_values(key_list[25], (D, D), (2 * D) ** -0.5, 0.1875),
        "b_proc": normal_values(key_list[26], (D,), 0.5, 3.0, (), jnp.float32),
        "w_proc_out": normal_values(key_list[27], (D, D), D ** -0.5, 0.25),
        "b_proc_out": normal_values(key_list[28], (D,), 0.5, 3.0, (), jnp.float32),
        "gain_proc": jnp.clip(1.0 + 0.15 * jax.random.normal(key_list[29], (D,), jnp.float32), 0.25, 1.75),
    }


def layer_norm(values, gain):
    center = values - lax.optimization_barrier(jnp.mean(values, -1, keepdims=True))
    spread = lax.optimization_barrier(jnp.mean(center * center, -1, keepdims=True))
    return center * lax.rsqrt(spread + 1e-05) * gain

def node_update(latent, summed, w_self, w_agg, bias, w_out, b_out, gain):
    preact = jnp.dot(latent, w_self, preferred_element_type=jnp.float32) + jnp.dot(summed, w_agg, preferred_element_type=jnp.float32) + bias
    hidden = jax.nn.silu(preact).astype(jnp.bfloat16)
    update = jnp.dot(hidden, w_out, preferred_element_type=jnp.float32) + b_out
    return (latent.astype(jnp.float32) + layer_norm(update, gain)).astype(jnp.bfloat16)

def reference(grid_lat, mesh_lat, enc_feat, enc_src, enc_dst, mesh_send, mesh_senders, mesh_recv, w_enc_grid, w_enc_feat, b_enc, w_enc_out, b_enc_out, w_node_self, w_node_agg, b_node, w_node_out, b_node_out, gain_node, w_edge_send, w_edge_recv, b_edge, w_edge_out, b_edge_out, w_proc_self, w_proc_agg, b_proc, w_proc_out, b_proc_out, gain_proc):

    def encode_band(band):
        grid_rows = lax.dynamic_slice_in_dim(grid_lat, band * G_DEV, G_DEV, 0)
        sources = lax.dynamic_slice_in_dim(enc_src, band * ENC_DEV, ENC_DEV, 0)
        targets = lax.dynamic_slice_in_dim(enc_dst, band * ENC_DEV, ENC_DEV, 0)
        features = lax.dynamic_slice_in_dim(enc_feat, band * ENC_DEV, ENC_DEV, 1)
        preact = jnp.dot(grid_rows[sources], w_enc_grid, preferred_element_type=jnp.float32)
        preact = preact + lax.dot_general(features, w_enc_feat, (((0,), (0,)), ((), ())), preferred_element_type=jnp.float32) + b_enc
        hidden = jax.nn.silu(preact).astype(jnp.bfloat16)
        messages = (jnp.dot(hidden, w_enc_out, preferred_element_type=jnp.float32) + b_enc_out).astype(jnp.bfloat16)
        partial_sum = jax.ops.segment_sum(messages.astype(jnp.float32), targets, num_segments=3 * M_DEV)
        return partial_sum.astype(jnp.bfloat16).reshape(3, M_DEV, D)
    band_part = lax.map(encode_band, jnp.arange(N_LAT, dtype=jnp.int32)).astype(jnp.float32)
    zero_band = jnp.zeros((1, M_DEV, D), jnp.float32)
    from_above = jnp.concatenate([band_part[1:, 0], zero_band], 0)
    from_below = jnp.concatenate([zero_band, band_part[:-1, 2]], 0)
    enc_agg = (band_part[:, 1] + from_above + from_below).reshape(MESH, D).astype(jnp.bfloat16)
    mesh_mid = node_update(mesh_lat, enc_agg, w_node_self, w_node_agg, b_node, w_node_out, b_node_out, gain_node)
    patch = jnp.arange(MEDGES, dtype=jnp.int32) // ME_DEV
    slot = jnp.maximum(mesh_senders - M_DEV, 0)
    source_patch = slot // CAP
    handed = mesh_send[source_patch, patch, slot % CAP]
    sender_rows = jnp.where(mesh_senders < M_DEV, patch * M_DEV + mesh_senders, source_patch * M_DEV + handed)
    receiver_rows = patch * M_DEV + mesh_recv
    preact = jnp.dot(mesh_mid[sender_rows], w_edge_send, preferred_element_type=jnp.float32)
    preact = preact + jnp.dot(mesh_mid[receiver_rows], w_edge_recv, preferred_element_type=jnp.float32) + b_edge
    hidden = jax.nn.silu(preact).astype(jnp.bfloat16)
    messages = (jnp.dot(hidden, w_edge_out, preferred_element_type=jnp.float32) + b_edge_out).astype(jnp.bfloat16)
    proc_agg = jax.ops.segment_sum(messages.astype(jnp.float32), receiver_rows, num_segments=MESH).astype(jnp.bfloat16)
    return node_update(mesh_mid, proc_agg, w_proc_self, w_proc_agg, b_proc, w_proc_out, b_proc_out, gain_proc)
```

```python
import functools

import jax
import jax.numpy as jnp
from jax import lax
from jax.experimental import pallas as pl
from jax.experimental.pallas import tpu as pltpu
from jax.sharding import PartitionSpec as P

F32 = jnp.float32
BF16 = jnp.bfloat16
LANES = 128
MESH_ID = pl.DeviceIdType.MESH
VMEM_BYTES = 48 * 1024 * 1024


def silu(x):
    half = 0.5 * x
    return half + half * jnp.tanh(half)


def dot(a, b):
    return jnp.dot(a, b, preferred_element_type=F32)


def dot_nt(a, b):
    return lax.dot_general(a, b, (((1,), (1,)), ((), ())), preferred_element_type=F32)


def dot_tn(a, b):
    return lax.dot_general(a, b, (((0,), (0,)), ((), ())), preferred_element_type=F32)


def split_dot(a, w):
    high = a.astype(BF16)
    low = (a - high.astype(F32)).astype(BF16)
    return dot(high, w) + dot(low, w)


def layer_norm(values, gain):
    center = values - jnp.mean(values, -1, keepdims=True)
    spread = jnp.mean(center * center, -1, keepdims=True)
    return center * lax.rsqrt(spread + 1e-05) * gain


def encode_kernel(
    src, grid_lat, feat, dst, w_grid, w_feat, b_enc, w_out, b_out, out, table, even, odd, acc, cnt
):
    grid_rows, width = grid_lat.shape
    edges = dst.shape[1]
    keys = out.shape[0]
    parts = width // LANES
    block = even.shape[0] // parts
    blocks = edges // block
    rows = 256

    def project(i, carry):
        p = dot(grid_lat[pl.ds(pl.multiple_of(i * rows, rows), rows), :], w_grid[...]) + b_enc[...]
        for j in range(parts):
            table[pl.ds(i * (rows * parts) + j, rows, stride=parts), :] = p[
                :, j * LANES : (j + 1) * LANES
            ]
        return carry

    lax.fori_loop(0, grid_rows // rows, project, 0)
    acc[...] = jnp.zeros_like(acc)
    cnt[...] = jnp.zeros_like(cnt)

    def gather(turn, held):
        base = turn * block
        for r in range(block):
            row = pl.multiple_of(src[base + r] * parts, parts)
            held[pl.ds(r * parts, parts), :] = table[pl.ds(row, parts), :]

    def compute(turn, held):
        cols = pl.ds(pl.multiple_of(turn * block, block), block)
        from_feat = dot_tn(feat[:, cols], w_feat[...])
        pieces = []
        for j in range(parts):
            x = held[pl.ds(j, block, stride=parts), :] + from_feat[:, j * LANES : (j + 1) * LANES]
            pieces.append(silu(x).astype(BF16))
        hidden = jnp.concatenate(pieces, axis=1)
        labels = lax.broadcasted_iota(jnp.int32, (keys, block), 0)
        hit = jnp.where(dst[:, cols] == labels, 1.0, 0.0).astype(F32)
        acc[...] += dot(hit.astype(BF16), hidden)
        total = hit[:, :LANES]
        for j in range(1, block // LANES):
            total = total + hit[:, j * LANES : (j + 1) * LANES]
        cnt[...] += total

    gather(0, even)

    def pair(k, carry):
        gather(2 * k + 1, odd)
        compute(2 * k, even)
        gather(jnp.minimum(2 * k + 2, blocks - 1), even)
        compute(2 * k + 1, odd)
        return carry

    lax.fori_loop(0, blocks // 2, pair, 0)
    count = jnp.sum(cnt[...], axis=1, keepdims=True)
    out[...] = (split_dot(acc[...], w_out[...]) + count * b_out[...]).astype(BF16)


def encode(grid_lat, feat, src, dst, w_grid, w_feat, b_enc, w_out, b_out, keys):
    width = grid_lat.shape[1]
    parts = width // LANES
    block = 256
    vmem = pl.BlockSpec(memory_space=pltpu.VMEM)
    edges = src.shape[0]
    return pl.pallas_call(
        encode_kernel,
        name="encode",
        out_shape=jax.ShapeDtypeStruct((keys, width), BF16),
        in_specs=[pl.BlockSpec(memory_space=pltpu.SMEM)] + [vmem] * 8,
        out_specs=vmem,
        scratch_shapes=[
            pltpu.VMEM((grid_lat.shape[0] * parts, LANES), F32),
            pltpu.VMEM((block * parts, LANES), F32),
            pltpu.VMEM((block * parts, LANES), F32),
            pltpu.VMEM((keys, width), F32),
            pltpu.VMEM((keys, LANES), F32),
        ],
        compiler_params=pltpu.CompilerParams(vmem_limit_bytes=VMEM_BYTES),
        cost_estimate=pl.CostEstimate(
            flops=2 * width * (grid_lat.shape[0] * width + edges * keys),
            bytes_accessed=2 * width * (grid_lat.shape[0] + 2 * width),
            transcendentals=edges * width,
        ),
    )(src, grid_lat, feat, dst, w_grid, w_feat, b_enc, w_out, b_out)


def process_kernel(
    peers,
    part,
    mesh_lat,
    mesh_send,
    senders,
    receivers,
    w_node_self_h,
    w_node_agg_h,
    w_node_out_h,
    w_edge_send_h,
    w_edge_recv_h,
    w_edge_out_h,
    w_proc_self_h,
    w_proc_agg_h,
    w_proc_out_h,
    b_node,
    b_node_out,
    gain_node,
    b_edge,
    b_edge_out,
    b_proc,
    b_proc_out,
    gain_proc,
    out,
    weights,
    below,
    above,
    outbox,
    inbox,
    chosen,
    hits_send,
    hits_recv,
    preact,
    weight_sem,
    halo_send_sem,
    halo_recv_sem,
    rows_send_sem,
    rows_recv_sem,
    own_sem,
):
    me = lax.axis_index("lat")
    patch, width = mesh_lat.shape
    half = width // 2
    cap = mesh_send.shape[2]
    two = 2 * cap
    edges = senders.shape[1]
    slots = peers * cap
    column = min(edges, 512)

    sources = (
        w_node_self_h,
        w_node_agg_h,
        w_node_out_h,
        w_edge_recv_h,
        w_edge_send_h,
        w_proc_self_h,
        w_edge_out_h,
        w_proc_agg_h,
        w_proc_out_h,
    )
    loads = [
        pltpu.make_async_copy(ref, weights.at[n], weight_sem.at[n]) for n, ref in enumerate(sources)
    ]
    for load in loads:
        load.start()

    barrier = pltpu.get_barrier_semaphore()

    def greet(k, carry):
        peer = lax.rem(me + k, peers)
        pl.semaphore_signal(barrier, inc=1, device_id={"lat": peer}, device_id_type=MESH_ID)
        return carry

    lax.fori_loop(1, peers, greet, 0)

    loads[0].wait()
    latent = mesh_lat[...]
    self_term = dot(latent, weights[0]) + b_node[...]

    pl.semaphore_wait(barrier, peers - 1)

    to_low = pltpu.make_async_remote_copy(
        src_ref=part.at[pl.ds(0, patch)],
        dst_ref=above,
        send_sem=halo_send_sem.at[0],
        recv_sem=halo_recv_sem.at[0],
        device_id={"lat": jnp.maximum(me - 1, 0)},
        device_id_type=MESH_ID,
    )
    to_high = pltpu.make_async_remote_copy(
        src_ref=part.at[pl.ds(2 * patch, patch)],
        dst_ref=below,
        send_sem=halo_send_sem.at[1],
        recv_sem=halo_recv_sem.at[1],
        device_id={"lat": jnp.minimum(me + 1, peers - 1)},
        device_id_type=MESH_ID,
    )

    @pl.when(me > 0)
    def _():
        to_low.start()

    @pl.when(me < peers - 1)
    def _():
        to_high.start()

    @pl.when(me == 0)
    def _():
        below[...] = jnp.zeros_like(below)

    @pl.when(me == peers - 1)
    def _():
        above[...] = jnp.zeros_like(above)

    picks = mesh_send[0].astype(F32)[:, None, :]
    row = lax.broadcasted_iota(jnp.int32, (peers, two, cap), 1)
    lane = lax.broadcasted_iota(jnp.int32, (peers, two, cap), 2)
    spread = jnp.where(lax.rem(row, cap) == lane, jnp.broadcast_to(picks, row.shape), 0.0)
    pick = jnp.sum(spread, axis=2, keepdims=True)
    side = lax.broadcasted_iota(jnp.int32, (peers, two, 1), 1) // cap
    pick = pick + (side * patch).astype(F32)
    spot = lax.broadcasted_iota(jnp.int32, (peers, two, 2 * patch), 2).astype(F32)
    chosen[...] = (
        jnp.where(spot == pick, 1.0, 0.0).reshape(peers * two, 2 * patch).astype(BF16)
    )

    labels = lax.broadcasted_iota(jnp.int32, (patch, edges), 0)
    hit = jnp.where(receivers[...] == labels, 1.0, 0.0).astype(F32)
    hits_recv[...] = hit.astype(BF16)
    count = jnp.sum(hit, axis=1, keepdims=True)
    for n in range((patch + slots) // patch):
        hits_send[n * patch : (n + 1) * patch, :] = jnp.where(
            senders[...] == labels + n * patch, 1.0, 0.0
        ).astype(BF16)

    @pl.when(me < peers - 1)
    def _():
        to_low.wait_recv()

    @pl.when(me > 0)
    def _():
        to_high.wait_recv()

    summed = (
        part[pl.ds(patch, patch), :].astype(F32) + above[...].astype(F32) + below[...].astype(F32)
    ).astype(BF16)
    loads[1].wait()
    hidden = silu(self_term + dot(summed, weights[1])).astype(BF16)
    loads[2].wait()
    update = dot(hidden, weights[2]) + b_node_out[...]
    mid = (latent.astype(F32) + layer_norm(update, gain_node[...])).astype(BF16)

    halves = jnp.concatenate([mid[:, :half], mid[:, half:]], axis=0)
    outbox[...] = dot(chosen[...], halves).astype(BF16)

    def send(k, carry):
        peer = lax.rem(me + k, peers)
        pltpu.make_async_remote_copy(
            src_ref=outbox.at[pl.ds(pl.multiple_of(peer * two, two), two)],
            dst_ref=inbox.at[pl.ds(pl.multiple_of(me * two, two), two)],
            send_sem=rows_send_sem,
            recv_sem=rows_recv_sem,
            device_id={"lat": peer},
            device_id_type=MESH_ID,
        ).start()
        return carry

    lax.fori_loop(1, peers, send, 0)
    mine = pl.ds(pl.multiple_of(me * two, two), two)
    own = pltpu.make_async_copy(outbox.at[mine], inbox.at[mine], own_sem)
    own.start()

    loads[3].wait()
    loads[4].wait()
    recv_table = (dot(mid, weights[3]) + b_edge[...]).T.astype(BF16)
    near_table = dot(mid, weights[4]).T.astype(BF16)
    local_table = jnp.concatenate([recv_table, near_table], axis=1)
    for n in range(edges // column):
        cols = slice(n * column, (n + 1) * column)
        preact[:, cols] = dot(
            local_table,
            jnp.concatenate([hits_recv[:, cols], hits_send[:patch, cols]], axis=0),
        )
    loads[5].wait()
    proc_term = dot(mid, weights[5]) + b_proc[...]

    own.wait()
    others = pl.ds(0, (peers - 1) * two)
    pltpu.make_async_copy(inbox.at[others], inbox.at[others], rows_recv_sem).wait()

    top = dot(inbox[...], weights[4, :half, :]).reshape(peers, two, width)
    low = dot(inbox[...], weights[4, half:, :]).reshape(peers, two, width)
    far_table = (top[:, :cap, :] + low[:, cap:, :]).reshape(slots, width).T.astype(BF16)
    gathered = jnp.zeros((patch, width), F32)
    for n in range(edges // column):
        cols = slice(n * column, (n + 1) * column)
        x = preact[:, cols] + dot(far_table, hits_send[patch:, cols])
        gathered = gathered + dot_nt(hits_recv[:, cols], silu(x).astype(BF16))
    loads[6].wait()
    summed = (split_dot(gathered, weights[6]) + count * b_edge_out[...]).astype(BF16)
    loads[7].wait()
    hidden = silu(proc_term + dot(summed, weights[7])).astype(BF16)
    loads[8].wait()
    update = dot(hidden, weights[8]) + b_proc_out[...]
    out[...] = (mid.astype(F32) + layer_norm(update, gain_proc[...])).astype(BF16)

    @pl.when(me > 0)
    def _():
        to_low.wait_send()

    @pl.when(me < peers - 1)
    def _():
        to_high.wait_send()

    pltpu.make_async_copy(outbox.at[others], outbox.at[others], rows_send_sem).wait()


def process(peers, part, mesh_lat, mesh_send, senders, receivers, mats, vectors):
    patch, width = mesh_lat.shape
    cap = mesh_send.shape[2]
    edges = senders.shape[1]
    slots = peers * cap
    vmem = pl.BlockSpec(memory_space=pltpu.VMEM)
    hbm = pl.BlockSpec(memory_space=pl.ANY)
    return pl.pallas_call(
        functools.partial(process_kernel, peers),
        name="process",
        out_shape=jax.ShapeDtypeStruct((patch, width), BF16),
        in_specs=[vmem] * 5 + [hbm] * len(mats) + [vmem] * len(vectors),
        out_specs=vmem,
        scratch_shapes=[
            pltpu.VMEM((len(mats), width, width), BF16),
            pltpu.VMEM((patch, width), BF16),
            pltpu.VMEM((patch, width), BF16),
            pltpu.VMEM((2 * slots, width // 2), BF16),
            pltpu.VMEM((2 * slots, width // 2), BF16),
            pltpu.VMEM((2 * slots, 2 * patch), BF16),
            pltpu.VMEM((patch + slots, edges), BF16),
            pltpu.VMEM((patch, edges), BF16),
            pltpu.VMEM((width, edges), F32),
            pltpu.SemaphoreType.DMA((len(mats),)),
            pltpu.SemaphoreType.DMA((2,)),
            pltpu.SemaphoreType.DMA((2,)),
            pltpu.SemaphoreType.DMA,
            pltpu.SemaphoreType.DMA,
            pltpu.SemaphoreType.DMA,
        ],
        compiler_params=pltpu.CompilerParams(
            collective_id=0, has_side_effects=True, vmem_limit_bytes=VMEM_BYTES
        ),
    )(part, mesh_lat, mesh_send, senders, receivers, *mats, *vectors)


def shards(
    grid_lat,
    mesh_lat,
    enc_feat,
    enc_src,
    enc_dst,
    mesh_send,
    mesh_senders,
    mesh_recv,
    w_enc_grid,
    w_enc_feat,
    b_enc,
    w_enc_out,
    b_enc_out,
    w_node_self,
    w_node_agg,
    b_node,
    w_node_out,
    b_node_out,
    gain_node,
    w_edge_send,
    w_edge_recv,
    b_edge,
    w_edge_out,
    b_edge_out,
    w_proc_self,
    w_proc_agg,
    b_proc,
    w_proc_out,
    b_proc_out,
    gain_proc,
):
    peers = lax.axis_size("lat")
    patch = mesh_lat.shape[0]

    def line(v):
        return v.reshape(1, -1)

    part = encode(
        grid_lat,
        enc_feat,
        enc_src,
        line(enc_dst),
        w_enc_grid,
        w_enc_feat,
        line(b_enc),
        w_enc_out,
        line(b_enc_out),
        3 * patch,
    )
    return process(
        peers,
        part,
        mesh_lat,
        mesh_send,
        line(mesh_senders),
        line(mesh_recv),
        (
            w_node_self,
            w_node_agg,
            w_node_out,
            w_edge_send,
            w_edge_recv,
            w_edge_out,
            w_proc_self,
            w_proc_agg,
            w_proc_out,
        ),
        tuple(
            line(v)
            for v in (
                b_node,
                b_node_out,
                gain_node,
                b_edge,
                b_edge_out,
                b_proc,
                b_proc_out,
                gain_proc,
            )
        ),
    )


def solution(mesh):
    rows = P(("groups", "lat"), None)
    flat = P(("groups", "lat"))
    placed = (
        rows,
        rows,
        P(None, ("groups", "lat")),
        flat,
        flat,
        P(("groups", "lat"), None, None),
        flat,
        flat,
    ) + (P(),) * 22
    return jax.shard_map(
        shards, mesh=mesh, in_specs=placed, out_specs=P(("groups", "lat"), None), check_vma=False
    )
```

```python
import functools

import jax
import jax.numpy as jnp
from jax import lax
from jax.experimental import pallas as pl
from jax.experimental.pallas import tpu as pltpu
from jax.sharding import PartitionSpec as P

F32 = jnp.float32
BF16 = jnp.bfloat16
LANES = 128
MESH_ID = pl.DeviceIdType.MESH
VMEM_BYTES = 63 * 1024 * 1024 + 512 * 1024
PIECES = 8
BLOCK = 512


def silu(x):
    half = 0.5 * x
    return half + half * jnp.tanh(half)


def dot(a, b):
    return jnp.dot(a, b, preferred_element_type=F32)


def dot_nt(a, b):
    return lax.dot_general(a, b, (((1,), (1,)), ((), ())), preferred_element_type=F32)


def dot_tn(a, b):
    return lax.dot_general(a, b, (((0,), (0,)), ((), ())), preferred_element_type=F32)


def split_dot(a, w):
    high = a.astype(BF16)
    low = (a - high.astype(F32)).astype(BF16)
    return dot(high, w) + dot(low, w)


def layer_norm(values, gain):
    center = values - jnp.mean(values, -1, keepdims=True)
    spread = jnp.mean(center * center, -1, keepdims=True)
    return center * lax.rsqrt(spread + 1e-05) * gain


def encode_kernel(
    src_h,
    grid_h,
    feat_h,
    dst_h,
    w_grid_h,
    w_feat_h,
    b_enc_h,
    w_out_h,
    b_out_h,
    out,
    src,
    grid_lat,
    feat,
    dst,
    w_grid,
    w_feat,
    b_enc,
    w_out,
    b_out,
    table,
    even,
    odd,
    acc,
    cnt,
    sems,
    grid_sems,
):
    grid_rows, width = grid_lat.shape
    edges = dst.shape[1]
    keys = out.shape[0]
    parts = width // LANES
    block = even.shape[0] // parts
    blocks = edges // block
    rows = grid_rows // PIECES

    def load(n, source, target):
        copy = pltpu.make_async_copy(source, target, sems.at[n])
        copy.start()
        return copy

    first = [load(0, w_grid_h, w_grid), load(1, b_enc_h, b_enc)]
    grid_loads = []
    for i in range(PIECES):
        piece = pl.ds(i * rows, rows)
        copy = pltpu.make_async_copy(grid_h.at[piece], grid_lat.at[piece], grid_sems.at[i])
        copy.start()
        grid_loads.append(copy)
    second = [
        load(2, src_h, src),
        load(3, feat_h, feat),
        load(4, dst_h, dst),
        load(5, w_feat_h, w_feat),
    ]
    third = [load(6, w_out_h, w_out), load(7, b_out_h, b_out)]

    acc[...] = jnp.zeros_like(acc)
    cnt[...] = jnp.zeros_like(cnt)
    for copy in first:
        copy.wait()
    for i in range(PIECES):
        grid_loads[i].wait()
        p = dot(grid_lat[i * rows : (i + 1) * rows, :], w_grid[...]) + b_enc[...]
        for j in range(parts):
            table[pl.ds(i * (rows * parts) + j, rows, stride=parts), :] = p[
                :, j * LANES : (j + 1) * LANES
            ]
    for copy in second:
        copy.wait()

    def gather(turn, held):
        base = turn * block
        for r in range(block):
            row = pl.multiple_of(src[base + r] * parts, parts)
            held[pl.ds(r * parts, parts), :] = table[pl.ds(row, parts), :]

    def compute(turn, held):
        cols = pl.ds(pl.multiple_of(turn * block, block), block)
        from_feat = dot_tn(feat[:, cols], w_feat[...])
        pieces = []
        for j in range(parts):
            x = held[pl.ds(j, block, stride=parts), :] + from_feat[:, j * LANES : (j + 1) * LANES]
            pieces.append(silu(x).astype(BF16))
        hidden = jnp.concatenate(pieces, axis=1)
        labels = lax.broadcasted_iota(jnp.int32, (keys, block), 0)
        hit = jnp.where(dst[:, cols] == labels, 1.0, 0.0).astype(F32)
        acc[...] += dot(hit.astype(BF16), hidden)
        total = hit[:, :LANES]
        for j in range(1, block // LANES):
            total = total + hit[:, j * LANES : (j + 1) * LANES]
        cnt[...] += total

    gather(0, even)

    def pair(k, carry):
        gather(2 * k + 1, odd)
        compute(2 * k, even)
        gather(jnp.minimum(2 * k + 2, blocks - 1), even)
        compute(2 * k + 1, odd)
        return carry

    lax.fori_loop(0, blocks // 2, pair, 0)
    for copy in third:
        copy.wait()
    count = jnp.sum(cnt[...], axis=1, keepdims=True)
    out[...] = (split_dot(acc[...], w_out[...]) + count * b_out[...]).astype(BF16)


def encode(grid_lat, feat, src, dst, w_grid, w_feat, b_enc, w_out, b_out, keys):
    width = grid_lat.shape[1]
    parts = width // LANES
    block = BLOCK
    edges = src.shape[0]
    operands = (src, grid_lat, feat, dst, w_grid, w_feat, b_enc, w_out, b_out)
    return pl.pallas_call(
        encode_kernel,
        name="encode",
        out_shape=jax.ShapeDtypeStruct((keys, width), BF16),
        in_specs=[pl.BlockSpec(memory_space=pl.ANY)] * len(operands),
        out_specs=pl.BlockSpec(memory_space=pltpu.VMEM),
        scratch_shapes=[pltpu.SMEM(src.shape, src.dtype)]
        + [pltpu.VMEM(a.shape, a.dtype) for a in operands[1:]]
        + [
            pltpu.VMEM((grid_lat.shape[0] * parts, LANES), F32),
            pltpu.VMEM((block * parts, LANES), F32),
            pltpu.VMEM((block * parts, LANES), F32),
            pltpu.VMEM((keys, width), F32),
            pltpu.VMEM((keys, LANES), F32),
            pltpu.SemaphoreType.DMA((8,)),
            pltpu.SemaphoreType.DMA((PIECES,)),
        ],
        compiler_params=pltpu.CompilerParams(vmem_limit_bytes=VMEM_BYTES),
        cost_estimate=pl.CostEstimate(
            flops=2 * width * (grid_lat.shape[0] * width + edges * keys),
            bytes_accessed=2 * width * (grid_lat.shape[0] + 2 * width),
            transcendentals=edges * width,
        ),
    )(*operands)


def process_kernel(
    peers,
    part_h,
    mesh_lat_h,
    mesh_send_h,
    senders_h,
    receivers_h,
    w_node_self_h,
    w_node_agg_h,
    w_node_out_h,
    w_edge_send_h,
    w_edge_recv_h,
    w_edge_out_h,
    w_proc_self_h,
    w_proc_agg_h,
    w_proc_out_h,
    b_node_h,
    b_node_out_h,
    gain_node_h,
    b_edge_h,
    b_edge_out_h,
    b_proc_h,
    b_proc_out_h,
    gain_proc_h,
    out,
    part,
    mesh_lat,
    mesh_send,
    senders,
    receivers,
    b_node,
    b_node_out,
    gain_node,
    b_edge,
    b_edge_out,
    b_proc,
    b_proc_out,
    gain_proc,
    weights,
    below,
    above,
    outbox,
    inbox,
    chosen,
    hits_send,
    hits_recv,
    preact,
    weight_sem,
    small_sem,
    halo_send_sem,
    halo_recv_sem,
    rows_send_sem,
    rows_recv_sem,
    own_sem,
):
    me = lax.axis_index("lat")
    patch, width = mesh_lat.shape
    half = width // 2
    cap = mesh_send.shape[2]
    two = 2 * cap
    edges = senders.shape[1]
    slots = peers * cap
    column = min(edges, 512)

    sources = (
        w_node_self_h,
        w_node_agg_h,
        w_node_out_h,
        w_edge_recv_h,
        w_edge_send_h,
        w_proc_self_h,
        w_edge_out_h,
        w_proc_agg_h,
        w_proc_out_h,
    )
    loads = [
        pltpu.make_async_copy(ref, weights.at[n], weight_sem.at[n]) for n, ref in enumerate(sources)
    ]
    small_pairs = (
        (part_h, part),
        (mesh_lat_h, mesh_lat),
        (mesh_send_h, mesh_send),
        (senders_h, senders),
        (receivers_h, receivers),
        (b_node_h, b_node),
        (b_node_out_h, b_node_out),
        (gain_node_h, gain_node),
        (b_edge_h, b_edge),
        (b_edge_out_h, b_edge_out),
        (b_proc_h, b_proc),
        (b_proc_out_h, b_proc_out),
        (gain_proc_h, gain_proc),
    )
    small_loads = [
        pltpu.make_async_copy(a, b, small_sem.at[n]) for n, (a, b) in enumerate(small_pairs)
    ]
    for load in small_loads:
        load.start()
    for load in loads:
        load.start()

    barrier = pltpu.get_barrier_semaphore()

    def greet(k, carry):
        peer = lax.rem(me + k, peers)
        pl.semaphore_signal(barrier, inc=1, device_id={"lat": peer}, device_id_type=MESH_ID)
        return carry

    lax.fori_loop(1, peers, greet, 0)

    for load in small_loads:
        load.wait()
    loads[0].wait()
    latent = mesh_lat[...]
    self_term = dot(latent, weights[0]) + b_node[...]

    pl.semaphore_wait(barrier, peers - 1)

    to_low = pltpu.make_async_remote_copy(
        src_ref=part.at[pl.ds(0, patch)],
        dst_ref=above,
        send_sem=halo_send_sem.at[0],
        recv_sem=halo_recv_sem.at[0],
        device_id={"lat": jnp.maximum(me - 1, 0)},
        device_id_type=MESH_ID,
    )
    to_high = pltpu.make_async_remote_copy(
        src_ref=part.at[pl.ds(2 * patch, patch)],
        dst_ref=below,
        send_sem=halo_send_sem.at[1],
        recv_sem=halo_recv_sem.at[1],
        device_id={"lat": jnp.minimum(me + 1, peers - 1)},
        device_id_type=MESH_ID,
    )

    @pl.when(me > 0)
    def _():
        to_low.start()

    @pl.when(me < peers - 1)
    def _():
        to_high.start()

    @pl.when(me == 0)
    def _():
        below[...] = jnp.zeros_like(below)

    @pl.when(me == peers - 1)
    def _():
        above[...] = jnp.zeros_like(above)

    picks = mesh_send[0].astype(F32)[:, None, :]
    row = lax.broadcasted_iota(jnp.int32, (peers, two, cap), 1)
    lane = lax.broadcasted_iota(jnp.int32, (peers, two, cap), 2)
    spread = jnp.where(lax.rem(row, cap) == lane, jnp.broadcast_to(picks, row.shape), 0.0)
    pick = jnp.sum(spread, axis=2, keepdims=True)
    side = lax.broadcasted_iota(jnp.int32, (peers, two, 1), 1) // cap
    pick = pick + (side * patch).astype(F32)
    spot = lax.broadcasted_iota(jnp.int32, (peers, two, 2 * patch), 2).astype(F32)
    chosen[...] = (
        jnp.where(spot == pick, 1.0, 0.0).reshape(peers * two, 2 * patch).astype(BF16)
    )

    labels = lax.broadcasted_iota(jnp.int32, (patch, edges), 0)
    hit = jnp.where(receivers[...] == labels, 1.0, 0.0).astype(F32)
    hits_recv[...] = hit.astype(BF16)
    count = jnp.sum(hit, axis=1, keepdims=True)
    for n in range((patch + slots) // patch):
        hits_send[n * patch : (n + 1) * patch, :] = jnp.where(
            senders[...] == labels + n * patch, 1.0, 0.0
        ).astype(BF16)

    @pl.when(me < peers - 1)
    def _():
        to_low.wait_recv()

    @pl.when(me > 0)
    def _():
        to_high.wait_recv()

    summed = (
        part[pl.ds(patch, patch), :].astype(F32) + above[...].astype(F32) + below[...].astype(F32)
    ).astype(BF16)
    loads[1].wait()
    hidden = silu(self_term + dot(summed, weights[1])).astype(BF16)
    loads[2].wait()
    update = dot(hidden, weights[2]) + b_node_out[...]
    mid = (latent.astype(F32) + layer_norm(update, gain_node[...])).astype(BF16)

    halves = jnp.concatenate([mid[:, :half], mid[:, half:]], axis=0)
    outbox[...] = dot(chosen[...], halves).astype(BF16)

    def send(k, carry):
        peer = lax.rem(me + k, peers)
        pltpu.make_async_remote_copy(
            src_ref=outbox.at[pl.ds(pl.multiple_of(peer * two, two), two)],
            dst_ref=inbox.at[pl.ds(pl.multiple_of(me * two, two), two)],
            send_sem=rows_send_sem,
            recv_sem=rows_recv_sem,
            device_id={"lat": peer},
            device_id_type=MESH_ID,
        ).start()
        return carry

    lax.fori_loop(1, peers, send, 0)
    mine = pl.ds(pl.multiple_of(me * two, two), two)
    own = pltpu.make_async_copy(outbox.at[mine], inbox.at[mine], own_sem)
    own.start()

    loads[3].wait()
    loads[4].wait()
    recv_table = (dot(mid, weights[3]) + b_edge[...]).T.astype(BF16)
    near_table = dot(mid, weights[4]).T.astype(BF16)
    local_table = jnp.concatenate([recv_table, near_table], axis=1)
    for n in range(edges // column):
        cols = slice(n * column, (n + 1) * column)
        preact[:, cols] = dot(
            local_table,
            jnp.concatenate([hits_recv[:, cols], hits_send[:patch, cols]], axis=0),
        )
    loads[5].wait()
    proc_term = dot(mid, weights[5]) + b_proc[...]

    own.wait()
    others = pl.ds(0, (peers - 1) * two)
    pltpu.make_async_copy(inbox.at[others], inbox.at[others], rows_recv_sem).wait()

    top = dot(inbox[...], weights[4, :half, :]).reshape(peers, two, width)
    low = dot(inbox[...], weights[4, half:, :]).reshape(peers, two, width)
    far_table = (top[:, :cap, :] + low[:, cap:, :]).reshape(slots, width).T.astype(BF16)
    gathered = jnp.zeros((patch, width), F32)
    for n in range(edges // column):
        cols = slice(n * column, (n + 1) * column)
        x = preact[:, cols] + dot(far_table, hits_send[patch:, cols])
        gathered = gathered + dot_nt(hits_recv[:, cols], silu(x).astype(BF16))
    loads[6].wait()
    summed = (split_dot(gathered, weights[6]) + count * b_edge_out[...]).astype(BF16)
    loads[7].wait()
    hidden = silu(proc_term + dot(summed, weights[7])).astype(BF16)
    loads[8].wait()
    update = dot(hidden, weights[8]) + b_proc_out[...]
    out[...] = (mid.astype(F32) + layer_norm(update, gain_proc[...])).astype(BF16)

    @pl.when(me > 0)
    def _():
        to_low.wait_send()

    @pl.when(me < peers - 1)
    def _():
        to_high.wait_send()

    pltpu.make_async_copy(outbox.at[others], outbox.at[others], rows_send_sem).wait()


def process(peers, part, mesh_lat, mesh_send, senders, receivers, mats, vectors):
    patch, width = mesh_lat.shape
    cap = mesh_send.shape[2]
    edges = senders.shape[1]
    slots = peers * cap
    vmem = pl.BlockSpec(memory_space=pltpu.VMEM)
    hbm = pl.BlockSpec(memory_space=pl.ANY)
    small = (part, mesh_lat, mesh_send, senders, receivers) + vectors
    return pl.pallas_call(
        functools.partial(process_kernel, peers),
        name="process",
        out_shape=jax.ShapeDtypeStruct((patch, width), BF16),
        in_specs=[hbm] * (5 + len(mats) + len(vectors)),
        out_specs=vmem,
        scratch_shapes=[pltpu.VMEM(a.shape, a.dtype) for a in small]
        + [
            pltpu.VMEM((len(mats), width, width), BF16),
            pltpu.VMEM((patch, width), BF16),
            pltpu.VMEM((patch, width), BF16),
            pltpu.VMEM((2 * slots, width // 2), BF16),
            pltpu.VMEM((2 * slots, width // 2), BF16),
            pltpu.VMEM((2 * slots, 2 * patch), BF16),
            pltpu.VMEM((patch + slots, edges), BF16),
            pltpu.VMEM((patch, edges), BF16),
            pltpu.VMEM((width, edges), F32),
            pltpu.SemaphoreType.DMA((len(mats),)),
            pltpu.SemaphoreType.DMA((len(small),)),
            pltpu.SemaphoreType.DMA((2,)),
            pltpu.SemaphoreType.DMA((2,)),
            pltpu.SemaphoreType.DMA,
            pltpu.SemaphoreType.DMA,
            pltpu.SemaphoreType.DMA,
        ],
        compiler_params=pltpu.CompilerParams(
            collective_id=0, has_side_effects=True, vmem_limit_bytes=VMEM_BYTES
        ),
    )(part, mesh_lat, mesh_send, senders, receivers, *mats, *vectors)


def shards(
    grid_lat,
    mesh_lat,
    enc_feat,
    enc_src,
    enc_dst,
    mesh_send,
    mesh_senders,
    mesh_recv,
    w_enc_grid,
    w_enc_feat,
    b_enc,
    w_enc_out,
    b_enc_out,
    w_node_self,
    w_node_agg,
    b_node,
    w_node_out,
    b_node_out,
    gain_node,
    w_edge_send,
    w_edge_recv,
    b_edge,
    w_edge_out,
    b_edge_out,
    w_proc_self,
    w_proc_agg,
    b_proc,
    w_proc_out,
    b_proc_out,
    gain_proc,
):
    peers = lax.axis_size("lat")
    patch = mesh_lat.shape[0]

    def line(v):
        return v.reshape(1, -1)

    part = encode(
        grid_lat,
        enc_feat,
        enc_src,
        line(enc_dst),
        w_enc_grid,
        w_enc_feat,
        line(b_enc),
        w_enc_out,
        line(b_enc_out),
        3 * patch,
    )
    return process(
        peers,
        part,
        mesh_lat,
        mesh_send,
        line(mesh_senders),
        line(mesh_recv),
        (
            w_node_self,
            w_node_agg,
            w_node_out,
            w_edge_send,
            w_edge_recv,
            w_edge_out,
            w_proc_self,
            w_proc_agg,
            w_proc_out,
        ),
        tuple(
            line(v)
            for v in (
                b_node,
                b_node_out,
                gain_node,
                b_edge,
                b_edge_out,
                b_proc,
                b_proc_out,
                gain_proc,
            )
        ),
    )


def solution(mesh):
    rows = P(("groups", "lat"), None)
    flat = P(("groups", "lat"))
    placed = (
        rows,
        rows,
        P(None, ("groups", "lat")),
        flat,
        flat,
        P(("groups", "lat"), None, None),
        flat,
        flat,
    ) + (P(),) * 22
    return jax.shard_map(
        shards, mesh=mesh, in_specs=placed, out_specs=P(("groups", "lat"), None), check_vma=False
    )
```

```python
import functools

import jax
import jax.numpy as jnp
from jax import lax
from jax.experimental import pallas as pl
from jax.experimental.pallas import tpu as pltpu
from jax.sharding import PartitionSpec as P

F32 = jnp.float32
BF16 = jnp.bfloat16
LANES = 128
MESH_ID = pl.DeviceIdType.MESH
VMEM_BYTES = 63 * 1024 * 1024 + 512 * 1024
PIECES = 8
BLOCK = 1024


def silu(x):
    half = 0.5 * x
    return half + half * jnp.tanh(half)


def dot(a, b):
    return jnp.dot(a, b, preferred_element_type=F32)


def dot_nt(a, b):
    return lax.dot_general(a, b, (((1,), (1,)), ((), ())), preferred_element_type=F32)


def dot_tn(a, b):
    return lax.dot_general(a, b, (((0,), (0,)), ((), ())), preferred_element_type=F32)


def split_dot(a, w):
    high = a.astype(BF16)
    low = (a - high.astype(F32)).astype(BF16)
    return dot(high, w) + dot(low, w)


def layer_norm(values, gain):
    center = values - jnp.mean(values, -1, keepdims=True)
    spread = jnp.mean(center * center, -1, keepdims=True)
    return center * lax.rsqrt(spread + 1e-05) * gain


def encode_kernel(
    src_h,
    grid_h,
    feat_h,
    dst_h,
    w_grid_h,
    w_feat_h,
    b_enc_h,
    w_out_h,
    b_out_h,
    out,
    src,
    grid_lat,
    feat,
    dst,
    w_grid,
    w_feat,
    b_enc,
    w_out,
    b_out,
    table,
    even,
    odd,
    acc,
    cnt,
    sems,
    grid_sems,
):
    grid_rows, width = grid_lat.shape
    edges = dst.shape[1]
    keys = out.shape[0]
    parts = width // LANES
    block = even.shape[0] // parts
    blocks = edges // block
    rows = grid_rows // PIECES

    def load(n, source, target):
        copy = pltpu.make_async_copy(source, target, sems.at[n])
        copy.start()
        return copy

    first = [load(0, w_grid_h, w_grid), load(1, b_enc_h, b_enc)]
    grid_loads = []
    for i in range(PIECES):
        piece = pl.ds(i * rows, rows)
        copy = pltpu.make_async_copy(grid_h.at[piece], grid_lat.at[piece], grid_sems.at[i])
        copy.start()
        grid_loads.append(copy)
    second = [
        load(2, src_h, src),
        load(3, feat_h, feat),
        load(4, dst_h, dst),
        load(5, w_feat_h, w_feat),
    ]
    third = [load(6, w_out_h, w_out), load(7, b_out_h, b_out)]

    acc[...] = jnp.zeros_like(acc)
    cnt[...] = jnp.zeros_like(cnt)
    for copy in first:
        copy.wait()
    for i in range(PIECES):
        grid_loads[i].wait()
        p = dot(grid_lat[i * rows : (i + 1) * rows, :], w_grid[...]) + b_enc[...]
        for j in range(parts):
            table[pl.ds(i * (rows * parts) + j, rows, stride=parts), :] = p[
                :, j * LANES : (j + 1) * LANES
            ]
    for copy in second:
        copy.wait()

    def gather(turn, held):
        base = turn * block
        for r in range(block):
            row = pl.multiple_of(src[base + r] * parts, parts)
            held[pl.ds(r * parts, parts), :] = table[pl.ds(row, parts), :]

    def compute(turn, held):
        cols = pl.ds(pl.multiple_of(turn * block, block), block)
        from_feat = dot_tn(feat[:, cols], w_feat[...])
        pieces = []
        for j in range(parts):
            x = held[pl.ds(j, block, stride=parts), :] + from_feat[:, j * LANES : (j + 1) * LANES]
            pieces.append(silu(x).astype(BF16))
        hidden = jnp.concatenate(pieces, axis=1)
        labels = lax.broadcasted_iota(jnp.int32, (keys, block), 0)
        hit = jnp.where(dst[:, cols] == labels, 1.0, 0.0).astype(F32)
        acc[...] += dot(hit.astype(BF16), hidden)
        total = hit[:, :LANES]
        for j in range(1, block // LANES):
            total = total + hit[:, j * LANES : (j + 1) * LANES]
        cnt[...] += total

    gather(0, even)

    def pair(k, carry):
        gather(2 * k + 1, odd)
        compute(2 * k, even)
        gather(jnp.minimum(2 * k + 2, blocks - 1), even)
        compute(2 * k + 1, odd)
        return carry

    lax.fori_loop(0, blocks // 2, pair, 0)
    for copy in third:
        copy.wait()
    count = jnp.sum(cnt[...], axis=1, keepdims=True)
    out[...] = (split_dot(acc[...], w_out[...]) + count * b_out[...]).astype(BF16)


def encode(grid_lat, feat, src, dst, w_grid, w_feat, b_enc, w_out, b_out, keys):
    width = grid_lat.shape[1]
    parts = width // LANES
    block = BLOCK
    edges = src.shape[0]
    operands = (src, grid_lat, feat, dst, w_grid, w_feat, b_enc, w_out, b_out)
    return pl.pallas_call(
        encode_kernel,
        name="encode",
        out_shape=jax.ShapeDtypeStruct((keys, width), BF16),
        in_specs=[pl.BlockSpec(memory_space=pl.ANY)] * len(operands),
        out_specs=pl.BlockSpec(memory_space=pltpu.VMEM),
        scratch_shapes=[pltpu.SMEM(src.shape, src.dtype)]
        + [pltpu.VMEM(a.shape, a.dtype) for a in operands[1:]]
        + [
            pltpu.VMEM((grid_lat.shape[0] * parts, LANES), F32),
            pltpu.VMEM((block * parts, LANES), F32),
            pltpu.VMEM((block * parts, LANES), F32),
            pltpu.VMEM((keys, width), F32),
            pltpu.VMEM((keys, LANES), F32),
            pltpu.SemaphoreType.DMA((8,)),
            pltpu.SemaphoreType.DMA((PIECES,)),
        ],
        compiler_params=pltpu.CompilerParams(vmem_limit_bytes=VMEM_BYTES),
        cost_estimate=pl.CostEstimate(
            flops=2 * width * (grid_lat.shape[0] * width + edges * keys),
            bytes_accessed=2 * width * (grid_lat.shape[0] + 2 * width),
            transcendentals=edges * width,
        ),
    )(*operands)


def process_kernel(
    peers,
    part_h,
    mesh_lat_h,
    mesh_send_h,
    senders_h,
    receivers_h,
    w_node_self_h,
    w_node_agg_h,
    w_node_out_h,
    w_edge_send_h,
    w_edge_recv_h,
    w_edge_out_h,
    w_proc_self_h,
    w_proc_agg_h,
    w_proc_out_h,
    b_node_h,
    b_node_out_h,
    gain_node_h,
    b_edge_h,
    b_edge_out_h,
    b_proc_h,
    b_proc_out_h,
    gain_proc_h,
    out,
    part,
    mesh_lat,
    mesh_send,
    senders,
    receivers,
    b_node,
    b_node_out,
    gain_node,
    b_edge,
    b_edge_out,
    b_proc,
    b_proc_out,
    gain_proc,
    weights,
    below,
    above,
    outbox,
    inbox,
    chosen,
    hits_send,
    hits_recv,
    preact,
    weight_sem,
    small_sem,
    halo_send_sem,
    halo_recv_sem,
    rows_send_sem,
    rows_recv_sem,
    own_sem,
):
    me = lax.axis_index("lat")
    patch, width = mesh_lat.shape
    half = width // 2
    cap = mesh_send.shape[1]
    two = 2 * cap
    edges = senders.shape[1]
    slots = peers * cap
    column = min(edges, 512)

    sources = (
        w_node_self_h,
        w_node_agg_h,
        w_node_out_h,
        w_edge_recv_h,
        w_edge_send_h,
        w_proc_self_h,
        w_edge_out_h,
        w_proc_agg_h,
        w_proc_out_h,
    )
    loads = [
        pltpu.make_async_copy(ref, weights.at[n], weight_sem.at[n]) for n, ref in enumerate(sources)
    ]
    small_pairs = (
        (part_h, part),
        (mesh_lat_h, mesh_lat),
        (mesh_send_h, mesh_send),
        (senders_h, senders),
        (receivers_h, receivers),
        (b_node_h, b_node),
        (b_node_out_h, b_node_out),
        (gain_node_h, gain_node),
        (b_edge_h, b_edge),
        (b_edge_out_h, b_edge_out),
        (b_proc_h, b_proc),
        (b_proc_out_h, b_proc_out),
        (gain_proc_h, gain_proc),
    )
    small_loads = [
        pltpu.make_async_copy(a, b, small_sem.at[n]) for n, (a, b) in enumerate(small_pairs)
    ]
    for load in small_loads:
        load.start()
    for load in loads:
        load.start()

    barrier = pltpu.get_barrier_semaphore()

    def greet(k, carry):
        peer = lax.rem(me + k, peers)
        pl.semaphore_signal(barrier, inc=1, device_id={"lat": peer}, device_id_type=MESH_ID)
        return carry

    lax.fori_loop(1, peers, greet, 0)

    for load in small_loads:
        load.wait()
    loads[0].wait()
    latent = mesh_lat[...]
    self_term = dot(latent, weights[0]) + b_node[...]

    pl.semaphore_wait(barrier, peers - 1)

    to_low = pltpu.make_async_remote_copy(
        src_ref=part.at[pl.ds(0, patch)],
        dst_ref=above,
        send_sem=halo_send_sem.at[0],
        recv_sem=halo_recv_sem.at[0],
        device_id={"lat": jnp.maximum(me - 1, 0)},
        device_id_type=MESH_ID,
    )
    to_high = pltpu.make_async_remote_copy(
        src_ref=part.at[pl.ds(2 * patch, patch)],
        dst_ref=below,
        send_sem=halo_send_sem.at[1],
        recv_sem=halo_recv_sem.at[1],
        device_id={"lat": jnp.minimum(me + 1, peers - 1)},
        device_id_type=MESH_ID,
    )

    @pl.when(me > 0)
    def _():
        to_low.start()

    @pl.when(me < peers - 1)
    def _():
        to_high.start()

    @pl.when(me == 0)
    def _():
        below[...] = jnp.zeros_like(below)

    @pl.when(me == peers - 1)
    def _():
        above[...] = jnp.zeros_like(above)

    unit = (
        lax.broadcasted_iota(jnp.int32, (cap, cap), 0)
        == lax.broadcasted_iota(jnp.int32, (cap, cap), 1)
    )
    unit = jnp.where(unit, 1.0, 0.0).astype(BF16)
    picks = dot_tn(mesh_send[0].astype(F32).astype(BF16), unit)[:, None, :]
    row = lax.broadcasted_iota(jnp.int32, (peers, two, cap), 1)
    lane = lax.broadcasted_iota(jnp.int32, (peers, two, cap), 2)
    spread = jnp.where(lax.rem(row, cap) == lane, jnp.broadcast_to(picks, row.shape), 0.0)
    pick = jnp.sum(spread, axis=2, keepdims=True)
    side = lax.broadcasted_iota(jnp.int32, (peers, two, 1), 1) // cap
    pick = pick + (side * patch).astype(F32)
    spot = lax.broadcasted_iota(jnp.int32, (peers, two, 2 * patch), 2).astype(F32)
    chosen[...] = (
        jnp.where(spot == pick, 1.0, 0.0).reshape(peers * two, 2 * patch).astype(BF16)
    )

    labels = lax.broadcasted_iota(jnp.int32, (patch, edges), 0)
    hit = jnp.where(receivers[...] == labels, 1.0, 0.0).astype(F32)
    hits_recv[...] = hit.astype(BF16)
    count = jnp.sum(hit, axis=1, keepdims=True)
    for n in range((patch + slots) // patch):
        hits_send[n * patch : (n + 1) * patch, :] = jnp.where(
            senders[...] == labels + n * patch, 1.0, 0.0
        ).astype(BF16)

    @pl.when(me < peers - 1)
    def _():
        to_low.wait_recv()

    @pl.when(me > 0)
    def _():
        to_high.wait_recv()

    summed = (
        part[pl.ds(patch, patch), :].astype(F32) + above[...].astype(F32) + below[...].astype(F32)
    ).astype(BF16)
    loads[1].wait()
    hidden = silu(self_term + dot(summed, weights[1])).astype(BF16)
    loads[2].wait()
    update = dot(hidden, weights[2]) + b_node_out[...]
    mid = (latent.astype(F32) + layer_norm(update, gain_node[...])).astype(BF16)

    halves = jnp.concatenate([mid[:, :half], mid[:, half:]], axis=0)
    outbox[...] = dot(chosen[...], halves).astype(BF16)

    def send(k, carry):
        peer = lax.rem(me + k, peers)
        pltpu.make_async_remote_copy(
            src_ref=outbox.at[pl.ds(pl.multiple_of(peer * two, two), two)],
            dst_ref=inbox.at[pl.ds(pl.multiple_of(me * two, two), two)],
            send_sem=rows_send_sem,
            recv_sem=rows_recv_sem,
            device_id={"lat": peer},
            device_id_type=MESH_ID,
        ).start()
        return carry

    lax.fori_loop(1, peers, send, 0)
    mine = pl.ds(pl.multiple_of(me * two, two), two)
    own = pltpu.make_async_copy(outbox.at[mine], inbox.at[mine], own_sem)
    own.start()

    loads[3].wait()
    loads[4].wait()
    recv_table = (dot(mid, weights[3]) + b_edge[...]).T.astype(BF16)
    near_table = dot(mid, weights[4]).T.astype(BF16)
    local_table = jnp.concatenate([recv_table, near_table], axis=1)
    for n in range(edges // column):
        cols = slice(n * column, (n + 1) * column)
        preact[:, cols] = dot(
            local_table,
            jnp.concatenate([hits_recv[:, cols], hits_send[:patch, cols]], axis=0),
        )
    loads[5].wait()
    proc_term = dot(mid, weights[5]) + b_proc[...]

    own.wait()
    others = pl.ds(0, (peers - 1) * two)
    pltpu.make_async_copy(inbox.at[others], inbox.at[others], rows_recv_sem).wait()

    top = dot(inbox[...], weights[4, :half, :]).reshape(peers, two, width)
    low = dot(inbox[...], weights[4, half:, :]).reshape(peers, two, width)
    far_table = (top[:, :cap, :] + low[:, cap:, :]).reshape(slots, width).T.astype(BF16)
    gathered = jnp.zeros((patch, width), F32)
    for n in range(edges // column):
        cols = slice(n * column, (n + 1) * column)
        x = preact[:, cols] + dot(far_table, hits_send[patch:, cols])
        gathered = gathered + dot_nt(hits_recv[:, cols], silu(x).astype(BF16))
    loads[6].wait()
    summed = (split_dot(gathered, weights[6]) + count * b_edge_out[...]).astype(BF16)
    loads[7].wait()
    hidden = silu(proc_term + dot(summed, weights[7])).astype(BF16)
    loads[8].wait()
    update = dot(hidden, weights[8]) + b_proc_out[...]
    out[...] = (mid.astype(F32) + layer_norm(update, gain_proc[...])).astype(BF16)

    @pl.when(me > 0)
    def _():
        to_low.wait_send()

    @pl.when(me < peers - 1)
    def _():
        to_high.wait_send()

    pltpu.make_async_copy(outbox.at[others], outbox.at[others], rows_send_sem).wait()


def process(peers, part, mesh_lat, mesh_send, senders, receivers, mats, vectors):
    patch, width = mesh_lat.shape
    cap = mesh_send.shape[1]
    edges = senders.shape[1]
    slots = peers * cap
    vmem = pl.BlockSpec(memory_space=pltpu.VMEM)
    hbm = pl.BlockSpec(memory_space=pl.ANY)
    small = (part, mesh_lat, mesh_send, senders, receivers) + vectors
    return pl.pallas_call(
        functools.partial(process_kernel, peers),
        name="process",
        out_shape=jax.ShapeDtypeStruct((patch, width), BF16),
        in_specs=[hbm] * (5 + len(mats) + len(vectors)),
        out_specs=vmem,
        scratch_shapes=[pltpu.VMEM(a.shape, a.dtype) for a in small]
        + [
            pltpu.VMEM((len(mats), width, width), BF16),
            pltpu.VMEM((patch, width), BF16),
            pltpu.VMEM((patch, width), BF16),
            pltpu.VMEM((2 * slots, width // 2), BF16),
            pltpu.VMEM((2 * slots, width // 2), BF16),
            pltpu.VMEM((2 * slots, 2 * patch), BF16),
            pltpu.VMEM((patch + slots, edges), BF16),
            pltpu.VMEM((patch, edges), BF16),
            pltpu.VMEM((width, edges), F32),
            pltpu.SemaphoreType.DMA((len(mats),)),
            pltpu.SemaphoreType.DMA((len(small),)),
            pltpu.SemaphoreType.DMA((2,)),
            pltpu.SemaphoreType.DMA((2,)),
            pltpu.SemaphoreType.DMA,
            pltpu.SemaphoreType.DMA,
            pltpu.SemaphoreType.DMA,
        ],
        compiler_params=pltpu.CompilerParams(
            collective_id=0, has_side_effects=True, vmem_limit_bytes=VMEM_BYTES
        ),
    )(part, mesh_lat, mesh_send, senders, receivers, *mats, *vectors)


def shards(
    grid_lat,
    mesh_lat,
    enc_feat,
    enc_src,
    enc_dst,
    mesh_send,
    mesh_senders,
    mesh_recv,
    w_enc_grid,
    w_enc_feat,
    b_enc,
    w_enc_out,
    b_enc_out,
    w_node_self,
    w_node_agg,
    b_node,
    w_node_out,
    b_node_out,
    gain_node,
    w_edge_send,
    w_edge_recv,
    b_edge,
    w_edge_out,
    b_edge_out,
    w_proc_self,
    w_proc_agg,
    b_proc,
    w_proc_out,
    b_proc_out,
    gain_proc,
):
    peers = lax.axis_size("lat")
    patch = mesh_lat.shape[0]

    def line(v):
        return v.reshape(1, -1)

    part = encode(
        grid_lat,
        enc_feat,
        enc_src,
        line(enc_dst),
        w_enc_grid,
        w_enc_feat,
        line(b_enc),
        w_enc_out,
        line(b_enc_out),
        3 * patch,
    )
    return process(
        peers,
        part,
        mesh_lat,
        jnp.swapaxes(mesh_send, 1, 2),
        line(mesh_senders),
        line(mesh_recv),
        (
            w_node_self,
            w_node_agg,
            w_node_out,
            w_edge_send,
            w_edge_recv,
            w_edge_out,
            w_proc_self,
            w_proc_agg,
            w_proc_out,
        ),
        tuple(
            line(v)
            for v in (
                b_node,
                b_node_out,
                gain_node,
                b_edge,
                b_edge_out,
                b_proc,
                b_proc_out,
                gain_proc,
            )
        ),
    )


def solution(mesh):
    rows = P(("groups", "lat"), None)
    flat = P(("groups", "lat"))
    placed = (
        rows,
        rows,
        P(None, ("groups", "lat")),
        flat,
        flat,
        P(("groups", "lat"), None, None),
        flat,
        flat,
    ) + (P(),) * 22
    return jax.shard_map(
        shards, mesh=mesh, in_specs=placed, out_specs=P(("groups", "lat"), None), check_vma=False
    )
```
